256 devices in a mesh: blk: 32 (over z, y_hi, core), member: 8 (over x, y_lo).
Axes of the slice: x: 4, y: 4 (y_hi: 2, y_lo: 2; y = y_hi * 2 + y_lo), z: 8, core: 2. Of those that a mesh axis runs over, the one named last changes fastest.
Arguments:
- frames: float32 [32, 4096, 1024], P('blk', 'member'), may hold values from -6 to 6
- targets: float32 [32, 4096, 1024], P('blk', 'member'), may hold values from -6 to 6
- w_first: float32 [32, 1024, 1024], P('blk', 'member'), may hold values from -6 to 6
- w_second: float32 [32, 1024, 1024], P('blk', 'member'), may hold values from -6 to 6
Outputs:
- new_first: float32 [32, 1024, 1024], P('blk', 'member')
- new_second: float32 [32, 1024, 1024], P('blk', 'member')
The draws below stay inside these ranges and needn't reach their ends.
All inputs are finite; a program needn't handle non-finite values.
Results may differ from the reference program's by a relative error of at most 0.000078.
Values sent between devices are 32-bit elements; how exact they have to be, the bound alone decides.
No kernel may reach another device: no remote copies, remote signals or barrier semaphores. Data moves between devices by JAX's collectives and lax.ppermute only.
A program may use at most 128 MiB of HBM per device.

```python
import jax
import jax.numpy as jnp
from jax import lax

D = 1024
H = 1024
GF = 4096
N_BLK = 32


def block_scale(key, shape, shards, least, top_value):
    def one(dim, blocks):
        heights = jax.random.uniform(jax.random.fold_in(jax.random.fold_in(key, 6), dim), (blocks,), jnp.float32, least / len(shards), top_value / len(shards))
        return jnp.repeat(jnp.exp(heights), shape[dim] // blocks).reshape((-1,) + (1,) * (len(shape) - dim - 1))

    gain = one(*shards[0])
    for cut in shards[1:]:
        gain = gain * one(*cut)
    return gain


def bell_draw(key, dims, deviation, reach, shards=(), kind=jnp.bfloat16):
    values = jax.random.normal(key, dims, jnp.float32) * deviation
    if len(shards) > 0:
        values = block_scale(key, dims, shards, -0.22, 0.18) * values
    return jnp.clip(values, min=-reach, max=reach).astype(kind)


def setup_inputs(seed: int = 0) -> dict:
    seeds = jax.random.split(jax.random.key(seed), 5)
    return {
        "frames": bell_draw(seeds[0], (N_BLK, GF, D), 1.0, 6.0, ((0, 32), (1, 8)), jnp.float32),
        "targets": bell_draw(seeds[1], (N_BLK, GF, D), 1.0, 6.0, ((0, 32), (1, 8)), jnp.float32),
        "w_first": bell_draw(seeds[2], (N_BLK, D, H), 1.0, 6.0, ((0, 32), (1, 8)), jnp.float32),
        "w_second": bell_draw(seeds[3], (N_BLK, H, D), 1.0, 6.0, ((0, 32), (1, 8)), jnp.float32),
    }


def group_grads(inputs, goal, first, second):
    scale_in = D ** -0.5
    scale_hid = H ** -0.5
    high = lax.Precision.HIGHEST
    pre_first = jnp.dot(inputs, first, precision=high, preferred_element_type=jnp.float32) * scale_in
    sig = jax.nn.sigmoid(pre_first)
    hidden = pre_first * sig
    slope = sig * (1.0 + pre_first * (1.0 - sig))
    output = jnp.dot(hidden, second, precision=high, preferred_element_type=jnp.float32) * scale_hid
    delta_out = (output - goal) / GF
    grad_second = jnp.dot(hidden.T, delta_out, precision=high, preferred_element_type=jnp.float32) * scale_hid
    back = jnp.dot(delta_out, second.T, precision=high, preferred_element_type=jnp.float32) * scale_hid
    delta_hidden = back * slope
    grad_first = jnp.dot(inputs.T, delta_hidden, precision=high, preferred_element_type=jnp.float32) * scale_in
    return grad_first, grad_second


def mixing(weights):
    return (jnp.roll(weights, 1, 0) + weights + jnp.roll(weights, -1, 0)) / 3.0


def reference(frames, targets, w_first, w_second):
    grad_first, grad_second = lax.map(lambda group: group_grads(*group), (frames, targets, w_first, w_second))
    new_first = mixing(w_first) - 300.0 * grad_first
    new_second = mixing(w_second) - 300.0 * grad_second
    return new_first, new_second
```

```python
import functools

import jax
import jax.numpy as jnp
from jax import lax
from jax.experimental import pallas as pl
from jax.experimental.pallas import tpu as pltpu
from jax.sharding import Mesh
from jax.sharding import PartitionSpec as P

RATE = 300.0
F32 = jnp.float32
BF16 = jnp.bfloat16
LANES = 256
CHUNKS = 2


def split(a):
    high = a.astype(BF16)
    return high, (a - high.astype(F32)).astype(BF16)


def dot(a, b, dims=((1,), (0,))):
    return lax.dot_general(a, b, (dims, ((), ())), preferred_element_type=F32)


def dot3(ah, al, bh, bl, dims=((1,), (0,))):
    return dot(ah, bl, dims) + dot(al, bh, dims) + dot(ah, bh, dims)


def place(at_ref, pieces, high_ref, low_ref):
    x, core = at_ref[0], at_ref[1]
    blocks = pieces[0].shape[0]
    for number, piece in enumerate(pieces):
        which, other = number % 5, number // 5
        part = lax.rem(core + other, 2)
        chip = lax.rem(x + (0, 3, 1, 2, 2)[which], 4)
        start = (chip * 2 + part) * blocks
        if which == 4:
            start = start + blocks // 2
        rows = piece.shape[0]
        start = pl.multiple_of(start, rows)
        high, low = split(piece[...])
        high_ref[pl.ds(start, rows), :] = high
        low_ref[pl.ds(start, rows), :] = low


def first_kernel(scale, at_ref, x_ref, *refs):
    pieces = refs[:10]
    hid_h, hid_l, hidt_h, hidt_l, slope, xt_h, xt_l, xh, xl, wh, wl = refs[10:]
    step = pl.program_id(0)

    @pl.when(step == 0)
    def _():
        high, low = split(x_ref[...])
        xh[...] = high
        xl[...] = low

    place(at_ref, pieces, wh, wl)
    pre = dot3(xh[...], xl[...], wh[...], wl[...]) * scale
    sig = 1.0 / (1.0 + jnp.exp(-pre))
    hidden = pre * sig
    slope[...] = sig * (1.0 + pre * (1.0 - sig))
    high, low = split(hidden)
    hid_h[...] = high
    hid_l[...] = low
    hidt_h[...] = high.T
    hidt_l[...] = low.T
    columns = pl.ds(pl.multiple_of(step * LANES, LANES), LANES)
    xt_h[...] = xh[:, columns].T
    xt_l[...] = xl[:, columns].T


def params(flops, moved):
    return dict(
        compiler_params=pltpu.CompilerParams(vmem_limit_bytes=48 * 2**20),
        cost_estimate=pl.CostEstimate(flops=flops, bytes_accessed=moved, transcendentals=0),
    )


def piece_specs(pieces):
    return [pl.BlockSpec((p.shape[0], LANES), lambda n, at: (0, n)) for p in pieces]


def first_layer(at, x, pieces, scale):
    rows, width = x.shape
    hid = pieces[0].shape[1]
    by_columns = pl.BlockSpec((rows, LANES), lambda n, at: (0, n))
    by_rows = pl.BlockSpec((LANES, rows), lambda n, at: (n, 0))
    return pl.pallas_call(
        functools.partial(first_kernel, scale),
        grid_spec=pltpu.PrefetchScalarGridSpec(
            num_scalar_prefetch=1,
            grid=(hid // LANES,),
            in_specs=[pl.BlockSpec((rows, width), lambda n, at: (0, 0))] + piece_specs(pieces),
            out_specs=[by_columns, by_columns, by_rows, by_rows, by_columns, by_rows, by_rows],
            scratch_shapes=[
                pltpu.VMEM((rows, width), BF16),
                pltpu.VMEM((rows, width), BF16),
                pltpu.VMEM((width, LANES), BF16),
                pltpu.VMEM((width, LANES), BF16),
            ],
        ),
        out_shape=[
            jax.ShapeDtypeStruct((rows, hid), BF16),
            jax.ShapeDtypeStruct((rows, hid), BF16),
            jax.ShapeDtypeStruct((hid, rows), BF16),
            jax.ShapeDtypeStruct((hid, rows), BF16),
            jax.ShapeDtypeStruct((rows, hid), F32),
            jax.ShapeDtypeStruct((width, rows), BF16),
            jax.ShapeDtypeStruct((width, rows), BF16),
        ],
        name="first_layer",
        **params(6 * rows * width * hid, 16 * 2**20),
    )(at, x, *pieces)


def second_kernel(scale, at_ref, hid_h, hid_l, *refs):
    pieces = refs[:10]
    out, wh, wl = refs[10:]
    place(at_ref, pieces, wh, wl)
    out[...] = dot3(hid_h[...], hid_l[...], wh[...], wl[...]) * scale


def second_layer(at, hid_h, hid_l, pieces, scale):
    rows, hid = hid_h.shape
    width = pieces[0].shape[1]
    whole = pl.BlockSpec((rows, hid), lambda n, at: (0, 0))
    weight = pl.BlockSpec((hid, LANES), lambda n, at: (0, n))
    return pl.pallas_call(
        functools.partial(second_kernel, scale),
        grid_spec=pltpu.PrefetchScalarGridSpec(
            num_scalar_prefetch=1,
            grid=(width // LANES,),
            in_specs=[whole, whole] + piece_specs(pieces),
            out_specs=[pl.BlockSpec((rows, LANES), lambda n, at: (0, n)), weight, weight],
        ),
        out_shape=[
            jax.ShapeDtypeStruct((rows, width), F32),
            jax.ShapeDtypeStruct((hid, width), BF16),
            jax.ShapeDtypeStruct((hid, width), BF16),
        ],
        name="second_layer",
        **params(6 * rows * width * hid, 12 * 2**20),
    )(at, hid_h, hid_l, *pieces)


def hand_out(at_ref, total, scratch, keep, send):
    core = at_ref[1]
    half = scratch.shape[0] // 2
    scratch[...] = total
    keep[0] = scratch[pl.ds(pl.multiple_of(core * half, half), half), :]
    send[0] = scratch[pl.ds(pl.multiple_of((1 - core) * half, half), half), :]


def delta_kernel(frames, scale, begun, at_ref, out, goal, hidt_h, hidt_l, wh, wl, *refs):
    back_in = refs[0] if begun else None
    keep, send, back, dh, dl, scratch = refs[1 if begun else 0 :]

    @pl.when(pl.program_id(0) == 0)
    def _():
        high, low = split((out[...] - goal[...]) / frames)
        dh[...] = high
        dl[...] = low

    total = dot3(hidt_h[...], hidt_l[...], dh[...], dl[...]) * scale
    hand_out(at_ref, total, scratch, keep, send)
    part = dot3(dh[...], dl[...], wh[...], wl[...], ((1,), (1,)))
    back[...] = part + back_in[...] if begun else part


def delta_and_second(at, number, out, goal, hidt_h, hidt_l, wh, wl, back_in, frames, scale):
    rows = out.shape[0]
    hid = hidt_h.shape[0]
    columns = goal.shape[1]
    blocks = hid // LANES
    begun = back_in is not None
    mine = lambda b, at: (b, 0)
    back_spec = pl.BlockSpec((rows, LANES), lambda b, at: (0, b))
    handed = pl.BlockSpec((1, LANES // 2, columns), lambda b, at: (lax.rem(b - at[0] + blocks, blocks), 0, 0))
    return pl.pallas_call(
        functools.partial(delta_kernel, frames, scale, begun),
        grid_spec=pltpu.PrefetchScalarGridSpec(
            num_scalar_prefetch=1,
            grid=(blocks,),
            in_specs=[
                pl.BlockSpec((rows, columns), lambda b, at: (0, number)),
                pl.BlockSpec((rows, columns), lambda b, at: (0, 0)),
                pl.BlockSpec((LANES, rows), mine),
                pl.BlockSpec((LANES, rows), mine),
                pl.BlockSpec((LANES, columns), lambda b, at: (b, number)),
                pl.BlockSpec((LANES, columns), lambda b, at: (b, number)),
            ]
            + ([back_spec] if begun else []),
            out_specs=[handed, handed, back_spec],
            scratch_shapes=[
                pltpu.VMEM((rows, columns), BF16),
                pltpu.VMEM((rows, columns), BF16),
                pltpu.VMEM((LANES, columns), F32),
            ],
        ),
        out_shape=[
            jax.ShapeDtypeStruct((blocks, LANES // 2, columns), F32),
            jax.ShapeDtypeStruct((blocks, LANES // 2, columns), F32),
            jax.ShapeDtypeStruct((rows, hid), F32),
        ],
        name="delta_and_second",
        **params(12 * rows * columns * hid, 12 * 2**20),
    )(at, out, goal, hidt_h, hidt_l, wh, wl, *([back_in] if begun else []))


def grad_first_kernel(scale_hid, scale_in, at_ref, back, slope, xt_h, xt_l, keep, send, dh, dl, scratch):
    @pl.when(pl.program_id(0) == 0)
    def _():
        high, low = split((back[...] * scale_hid) * slope[...])
        dh[...] = high
        dl[...] = low

    total = dot3(xt_h[...], xt_l[...], dh[...], dl[...]) * scale_in
    hand_out(at_ref, total, scratch, keep, send)


def grad_first(at, number, back, slope, xt_h, xt_l, scale_hid, scale_in):
    rows, hid = back.shape
    width = xt_h.shape[0]
    columns = hid // CHUNKS
    blocks = width // LANES
    by_columns = pl.BlockSpec((rows, columns), lambda b, at: (0, number))
    by_rows = pl.BlockSpec((LANES, rows), lambda b, at: (b, 0))
    handed = pl.BlockSpec((1, LANES // 2, columns), lambda b, at: (lax.rem(b - at[0] + blocks, blocks), 0, 0))
    return pl.pallas_call(
        functools.partial(grad_first_kernel, scale_hid, scale_in),
        grid_spec=pltpu.PrefetchScalarGridSpec(
            num_scalar_prefetch=1,
            grid=(blocks,),
            in_specs=[by_columns, by_columns, by_rows, by_rows],
            out_specs=[handed, handed],
            scratch_shapes=[
                pltpu.VMEM((rows, columns), BF16),
                pltpu.VMEM((rows, columns), BF16),
                pltpu.VMEM((LANES, columns), F32),
            ],
        ),
        out_shape=[
            jax.ShapeDtypeStruct((blocks, LANES // 2, columns), F32),
            jax.ShapeDtypeStruct((blocks, LANES // 2, columns), F32),
        ],
        name="grad_first",
        **params(6 * rows * columns * width, 6 * 2**20),
    )(at, back, slope, xt_h, xt_l)


def along_x(a, by):
    n = lax.axis_size("x")
    return lax.ppermute(a, "x", [(i, (i + by) % n) for i in range(n)])


def to_other_core(a):
    return lax.ppermute(a, "core", [(0, 1), (1, 0)])


def regroup(a):
    return lax.ppermute(a, ("core", "y_lo"), [(0, 0), (1, 2), (2, 1), (3, 3)])


def next_door(a):
    n = lax.axis_size("z") * 4
    pairs = [(i, i + 1) for i in range(1, n, 2)]
    pairs = [(i, j % n) for i, j in pairs]
    return lax.ppermute(a, ("z", "y_hi", "y_lo"), pairs + [(j, i) for i, j in pairs])


def gathered(own):
    half = own.shape[0] // 2
    left, right = along_x(own, 1), along_x(own, -1)
    top = along_x(left[:half], 1)
    bottom = along_x(right[half:], -1)
    pieces = [own, left, right, top, bottom]
    return pieces + [to_other_core(p) for p in pieces]


def summed(keep, send):
    half = keep.shape[1] // 2
    total = keep + to_other_core(send)
    from_left = along_x(total[2, :half], 1)
    from_right = along_x(total[2, half:], -1)
    to_right = jnp.concatenate([total[1, :half] + from_left, total[1, half:]], 0)
    to_left = jnp.concatenate([total[3, :half], total[3, half:] + from_right], 0)
    return total[0] + along_x(to_right, 1) + along_x(to_left, -1)


def body(frames, targets, w_first, w_second):
    inputs, goal = frames[0], targets[0]
    own_first, own_second = w_first[0], w_second[0]
    total_frames = inputs.shape[0] * 8
    width, hid = inputs.shape[1], own_first.shape[1]
    scale_in, scale_hid = width ** (-0.5), hid ** (-0.5)
    columns = width // CHUNKS
    at = jnp.stack([lax.axis_index("x"), lax.axis_index("core")]).astype(jnp.int32)

    mine_first = regroup(own_first)
    mine_second = regroup(own_second)
    x = regroup(inputs)
    goals = [regroup(goal[:, j * columns : (j + 1) * columns]) for j in range(CHUNKS)]
    pieces_first = gathered(mine_first)
    pieces_second = gathered(mine_second)
    near_first = (own_first + to_other_core(own_first)) / 3.0
    near_second = (own_second + to_other_core(own_second)) / 3.0
    far_first = next_door(mine_first) / 3.0
    far_second = next_door(mine_second) / 3.0

    hid_h, hid_l, hidt_h, hidt_l, slope, xt_h, xt_l = first_layer(at, x, pieces_first, scale_in)
    out, wh, wl = second_layer(at, hid_h, hid_l, pieces_second, scale_hid)
    back = None
    new_second = []
    for j in range(CHUNKS):
        keep, send, back = delta_and_second(
            at, j, out, goals[j], hidt_h, hidt_l, wh, wl, back, total_frames, scale_hid
        )
        new_second.append(summed(keep, send))
    new_first = []
    for j in range(CHUNKS):
        keep, send = grad_first(at, j, back, slope, xt_h, xt_l, scale_hid, scale_in)
        new_first.append(summed(keep, send))
    updates_second = jnp.concatenate(new_second, 1)
    new_second = near_second + regroup(far_second - RATE * updates_second)
    parts = []
    for j in range(CHUNKS):
        cut = slice(j * columns, (j + 1) * columns)
        parts.append(near_first[:, cut] + regroup(far_first[:, cut] - RATE * new_first[j]))
    return (jnp.concatenate(parts, 1)[None], new_second[None])


def solution(mesh):
    torus = Mesh(
        mesh.devices.reshape(mesh.shape["blk"] // 4, 2, 2, 4, 2), ("z", "y_hi", "core", "x", "y_lo")
    )
    spec = P(("z", "y_hi", "core"), ("x", "y_lo"), None)
    return jax.shard_map(
        body, mesh=torus, in_specs=(spec,) * 4, out_specs=(spec, spec), check_vma=False
    )
```

```python
import functools

import jax
import jax.numpy as jnp
from jax import lax
from jax.experimental import pallas as pl
from jax.experimental.pallas import tpu as pltpu
from jax.sharding import Mesh
from jax.sharding import PartitionSpec as P

RATE = 300.0
F32 = jnp.float32
BF16 = jnp.bfloat16
TILE = 256

VMEM = pl.BlockSpec(memory_space=pltpu.VMEM)
SMEM = pl.BlockSpec(memory_space=pltpu.SMEM)
HBM = pl.BlockSpec(memory_space=pltpu.HBM)


def split(a):
    high = a.astype(BF16)
    return high, (a - high.astype(F32)).astype(BF16)


def dot(a, b, dims=((1,), (0,))):
    return lax.dot_general(a, b, (dims, ((), ())), preferred_element_type=F32)


def dot3(ah, al, bh, bl, dims=((1,), (0,))):
    return dot(ah, bl, dims) + dot(al, bh, dims) + dot(ah, bh, dims)


def params(flops, moved):
    return dict(
        compiler_params=pltpu.CompilerParams(vmem_limit_bytes=30 * 2**20),
        cost_estimate=pl.CostEstimate(flops=flops, bytes_accessed=moved, transcendentals=0),
    )


class Taken:
    def __init__(self, at_ref, own, sent, into, sem):
        self.wait = pltpu.make_async_copy(own, into, sem).wait

        @pl.when(at_ref[2] == 1)
        def _():
            pltpu.make_async_copy(sent, into, sem).start()

        @pl.when(at_ref[2] == 0)
        def _():
            pltpu.make_async_copy(own, into, sem).start()


def place(at_ref, gathered, high_ref, low_ref):
    x, core = at_ref[0], at_ref[1]
    way = 1 - 2 * core
    rows = gathered.shape[1]
    for number in range(8):
        step, other = number % 4, number // 4
        part = core if other == 0 else 1 - core
        chip = lax.rem(x - way * step + 4 if other == 0 else x + way * step + 4, 4)
        start = pl.multiple_of((chip * 2 + part) * rows, rows)
        high, low = split(gathered[number])
        high_ref[pl.ds(start, rows), :] = high
        low_ref[pl.ds(start, rows), :] = low


def fetch_weights(mine, theirs, raw, sem):
    copies = [
        pltpu.make_async_copy(a, raw.at[pl.ds(4 * i, 4)], sem.at[i]) for i, a in enumerate((mine, theirs))
    ]
    for copy in copies:
        copy.start()
    return copies


def first_kernel(scale, at_ref, own, sent, mine, theirs, *refs):
    hid_h, hid_l, hidt_h, hidt_l, slope, xt_h, xt_l, x, xh, xl, raw, wh, wl, sem = refs
    width = x.shape[1]
    taken = Taken(at_ref, own.at[:, pl.ds(0, width)], sent.at[:, pl.ds(0, width)], x, sem.at[2])
    copies = fetch_weights(mine, theirs, raw, sem)
    taken.wait()
    high, low = split(x[...])
    xh[...] = high
    xl[...] = low
    for copy in copies:
        copy.wait()
    place(at_ref, raw, wh, wl)
    for n in range(slope.shape[1] // TILE):
        cut = slice(n * TILE, (n + 1) * TILE)
        pre = dot3(xh[...], xl[...], wh[:, cut], wl[:, cut]) * scale
        sig = 1.0 / (1.0 + jnp.exp(-pre))
        hidden = pre * sig
        slope[:, cut] = sig * (1.0 + pre * (1.0 - sig))
        high, low = split(hidden)
        hid_h[:, cut] = high
        hid_l[:, cut] = low
        hidt_h[cut, :] = high.T
        hidt_l[cut, :] = low.T
        xt_h[cut, :] = xh[:, cut].T
        xt_l[cut, :] = xl[:, cut].T


def first_layer(at, own, sent, mine, theirs, scale):
    rows, width = own.shape[0], 8 * mine.shape[1]
    hid = mine.shape[2]
    shapes = [((rows, hid), BF16)] * 2 + [((hid, rows), BF16)] * 2
    shapes += [((rows, hid), F32)] + [((width, rows), BF16)] * 2
    return pl.pallas_call(
        functools.partial(first_kernel, scale),
        in_specs=[SMEM] + [HBM] * 4,
        out_specs=[VMEM] * len(shapes),
        out_shape=[jax.ShapeDtypeStruct(*s) for s in shapes],
        scratch_shapes=[
            pltpu.VMEM((rows, width), F32),
            pltpu.VMEM((rows, width), BF16),
            pltpu.VMEM((rows, width), BF16),
            pltpu.VMEM((8,) + mine.shape[1:], F32),
            pltpu.VMEM((width, hid), BF16),
            pltpu.VMEM((width, hid), BF16),
            pltpu.SemaphoreType.DMA((3,)),
        ],
        name="first_layer",
        **params(6 * rows * width * hid, 16 * 2**20),
    )(at, own, sent, mine, theirs)


def second_kernel(scale, at_ref, hid_h, hid_l, mine, theirs, out, wh, wl, raw, sem):
    for copy in fetch_weights(mine, theirs, raw, sem):
        copy.wait()
    place(at_ref, raw, wh, wl)
    for n in range(out.shape[1] // TILE):
        cut = slice(n * TILE, (n + 1) * TILE)
        out[:, cut] = dot3(hid_h[...], hid_l[...], wh[:, cut], wl[:, cut]) * scale


def second_layer(at, hid_h, hid_l, mine, theirs, scale):
    rows, hid = hid_h.shape
    width = mine.shape[2]
    return pl.pallas_call(
        functools.partial(second_kernel, scale),
        in_specs=[SMEM, VMEM, VMEM, HBM, HBM],
        out_specs=[VMEM] * 3,
        out_shape=[
            jax.ShapeDtypeStruct((rows, width), F32),
            jax.ShapeDtypeStruct((hid, width), BF16),
            jax.ShapeDtypeStruct((hid, width), BF16),
        ],
        scratch_shapes=[pltpu.VMEM((8,) + mine.shape[1:], F32), pltpu.SemaphoreType.DMA((2,))],
        name="second_layer",
        **params(6 * rows * width * hid, 12 * 2**20),
    )(at, hid_h, hid_l, mine, theirs)


def hand_out(at_ref, total, keep, send):
    x, core = at_ref[0], at_ref[1]
    way = 1 - 2 * core
    half = keep.shape[1]
    for k in range(4):
        ahead = lax.rem(x + way * k + 4, 4) * 2
        behind = lax.rem(x - way * k + 4, 4) * 2
        keep[k] = total[pl.ds(pl.multiple_of((ahead + core) * half, half), half), :]
        send[k] = total[pl.ds(pl.multiple_of((behind + 1 - core) * half, half), half), :]


def delta_kernel(frames, scale, begun, start, at_ref, out, own, sent, hidt_h, hidt_l, wh, wl, *refs):
    back_in = refs[0] if begun else None
    keep, send, back, goal, dh, dl, total, sem = refs[1 if begun else 0 :]
    columns = goal.shape[1]
    cut = slice(start, start + columns)
    there = pl.ds(start, columns)
    Taken(at_ref, own.at[:, there], sent.at[:, there], goal, sem).wait()
    high, low = split((out[:, cut] - goal[...]) / frames)
    dh[...] = high
    dl[...] = low
    for n in range(columns // TILE):
        part = slice(n * TILE, (n + 1) * TILE)
        total[:, part] = dot3(hidt_h[...], hidt_l[...], dh[:, part], dl[:, part]) * scale
    hand_out(at_ref, total, keep, send)
    for n in range(back.shape[1] // TILE):
        part = slice(n * TILE, (n + 1) * TILE)
        more = dot3(dh[...], dl[...], wh[part, cut], wl[part, cut], ((1,), (1,)))
        back[:, part] = back_in[:, part] + more if begun else more


def delta_and_second(at, start, columns, out, own, sent, hidt_h, hidt_l, wh, wl, back_in, frames, scale):
    rows = out.shape[0]
    hid = hidt_h.shape[0]
    begun = back_in is not None
    return pl.pallas_call(
        functools.partial(delta_kernel, frames, scale, begun, start),
        in_specs=[SMEM, VMEM, HBM, HBM] + [VMEM] * (5 if begun else 4),
        out_specs=[VMEM] * 3,
        out_shape=[
            jax.ShapeDtypeStruct((4, hid // 8, columns), F32),
            jax.ShapeDtypeStruct((4, hid // 8, columns), F32),
            jax.ShapeDtypeStruct((rows, hid), F32),
        ],
        scratch_shapes=[
            pltpu.VMEM((rows, columns), F32),
            pltpu.VMEM((rows, columns), BF16),
            pltpu.VMEM((rows, columns), BF16),
            pltpu.VMEM((hid, columns), F32),
            pltpu.SemaphoreType.DMA,
        ],
        name="delta_and_second",
        **params(12 * rows * columns * hid, 12 * 2**20),
    )(at, out, own, sent, hidt_h, hidt_l, wh, wl, *([back_in] if begun else []))


def grad_first_kernel(scale_hid, scale_in, start, at_ref, back, slope, xt_h, xt_l, keep, send, total):
    for n in range(total.shape[1] // TILE):
        part = slice(n * TILE, (n + 1) * TILE)
        cut = slice(start + n * TILE, start + (n + 1) * TILE)
        high, low = split((back[:, cut] * scale_hid) * slope[:, cut])
        total[:, part] = dot3(xt_h[...], xt_l[...], high, low) * scale_in
    hand_out(at_ref, total, keep, send)


def grad_first(at, start, columns, back, slope, xt_h, xt_l, scale_hid, scale_in):
    rows, hid = back.shape
    width = xt_h.shape[0]
    return pl.pallas_call(
        functools.partial(grad_first_kernel, scale_hid, scale_in, start),
        in_specs=[SMEM] + [VMEM] * 4,
        out_specs=[VMEM] * 2,
        out_shape=[jax.ShapeDtypeStruct((4, width // 8, columns), F32)] * 2,
        scratch_shapes=[pltpu.VMEM((width, columns), F32)],
        name="grad_first",
        **params(6 * rows * columns * width, 6 * 2**20),
    )(at, back, slope, xt_h, xt_l)


def round_x(a):
    n = lax.axis_size("x")
    pairs = [(i, (i + 1) % n) for i in range(n)] + [(n + i, n + (i - 1) % n) for i in range(n)]
    return lax.ppermute(a, ("core", "x"), pairs)


def to_other_core(a):
    return lax.ppermute(a, "core", [(0, 1), (1, 0)])


def across(a):
    return lax.ppermute(a, ("core", "y_lo"), [(1, 2), (2, 1)])


def next_door(a):
    n = lax.axis_size("z") * 4
    pairs = [(i, (i + 1) % n) for i in range(1, n, 2)]
    return lax.ppermute(a, ("z", "y_hi", "y_lo"), pairs + [(j, i) for i, j in pairs])


def after(value, *others):
    return lax.optimization_barrier((value, *others))[0]


def body(frames, targets, w_first, w_second):
    inputs, goal = frames[0], targets[0]
    own_first, own_second = w_first[0], w_second[0]
    total_frames = inputs.shape[0] * 8
    width, hid = inputs.shape[1], own_first.shape[1]
    scale_in, scale_hid = width ** (-0.5), hid ** (-0.5)
    half = width // 2
    core = lax.axis_index("core")
    moves = core != lax.axis_index("y_lo")
    at = jnp.stack([lax.axis_index("x"), core, moves]).astype(jnp.int32)

    got_first, got_second = across(own_first), across(own_second)
    ring = [jnp.where(moves, got_first, own_first)]
    ring2 = [jnp.where(moves, got_second, own_second)]
    sent = across(after(inputs, got_second))
    sent_goal = across(after(goal, got_second))

    for _ in range(2):
        ring.append(round_x(ring[-1]))
        ring2.append(round_x(ring2[-1]))
    far_first = next_door(ring[0])
    ring.append(round_x(ring[2]))
    ring2.append(round_x(after(ring2[2], sent)))
    mine = jnp.stack(ring)
    mine2 = jnp.stack(ring2)
    theirs = to_other_core(mine)
    mine2, far_first, sent_goal = lax.optimization_barrier((mine2, far_first, sent_goal))
    theirs2 = to_other_core(mine2)

    hid_h, hid_l, hidt_h, hidt_l, slope, xt_h, xt_l = first_layer(at, inputs, sent, mine, theirs, scale_in)
    out, wh, wl = second_layer(at, hid_h, hid_l, mine2, theirs2, scale_hid)

    def delta(start, own, sent, back):
        keep, send, back = delta_and_second(
            at, start, half, out, own, sent, hidt_h, hidt_l, wh, wl, back, total_frames, scale_hid
        )
        return keep, to_other_core(send), back

    def first(start, back):
        keep, send = grad_first(at, start, half, back, slope, xt_h, xt_l, scale_hid, scale_in)
        return keep, to_other_core(send)

    def term(keeps, sents, k):
        return jnp.concatenate([a[k] + b[k] for a, b in zip(keeps, sents)], 1)

    keep0, sent0, back = delta(0, goal, sent_goal, None)
    keep1, sent1, back = delta(half, goal, sent_goal, back)
    far_second = next_door(after(ring2[0], back))
    second = (keep0, keep1), (sent0, sent1)
    m = term(*second, 3)
    keep2, sent2 = first(0, after(back, m))
    keep3, sent3 = first(half, back)
    firsts = (keep2, keep3), (sent2, sent3)
    p = term(*firsts, 3)
    m = round_x(m) + term(*second, 2)
    p = round_x(p) + term(*firsts, 2)
    m = round_x(m) + term(*second, 1)
    p = round_x(after(p, far_second)) + term(*firsts, 1)
    m = round_x(m) + term(*second, 0)
    update_second = far_second / 3.0 - RATE * m
    near_first, near_second = ((w + to_other_core(after(w, back))) / 3.0 for w in (own_first, own_second))
    p, update_second, near_first, near_second = lax.optimization_barrier((p, update_second, near_first, near_second))
    p = round_x(p) + term(*firsts, 0)
    update_first = far_first / 3.0 - RATE * p
    new = []
    for near, update in ((near_first, update_first), (near_second, update_second)):
        new.append((near + jnp.where(moves, across(update), update))[None])
    return tuple(new)


def solution(mesh):
    torus = Mesh(
        mesh.devices.reshape(mesh.shape["blk"] // 4, 2, 2, 4, 2), ("z", "y_hi", "core", "x", "y_lo")
    )
    spec = P(("z", "y_hi", "core"), ("x", "y_lo"), None)
    return jax.shard_map(
        body, mesh=torus, in_specs=(spec,) * 4, out_specs=(spec, spec), check_vma=False
    )
```

```python
import functools

import jax
import jax.numpy as jnp
from jax import lax
from jax.experimental import pallas as pl
from jax.experimental.pallas import tpu as pltpu
from jax.sharding import Mesh
from jax.sharding import PartitionSpec as P

RATE = 300.0
F32 = jnp.float32
BF16 = jnp.bfloat16
TILE = 256

VMEM = pl.BlockSpec(memory_space=pltpu.VMEM)
SMEM = pl.BlockSpec(memory_space=pltpu.SMEM)
HBM = pl.BlockSpec(memory_space=pltpu.HBM)


def split(a):
    high = a.astype(BF16)
    return high, (a - high.astype(F32)).astype(BF16)


def dot(a, b, dims=((1,), (0,))):
    return lax.dot_general(a, b, (dims, ((), ())), preferred_element_type=F32)


def dot3(ah, al, bh, bl, dims=((1,), (0,))):
    return dot(ah, bl, dims) + dot(al, bh, dims) + dot(ah, bh, dims)


def params(flops, moved):
    return dict(
        compiler_params=pltpu.CompilerParams(vmem_limit_bytes=30 * 2**20),
        cost_estimate=pl.CostEstimate(flops=flops, bytes_accessed=moved, transcendentals=0),
    )


class Taken:
    def __init__(self, at_ref, own, sent, into, sem):
        self.wait = pltpu.make_async_copy(own, into, sem).wait

        @pl.when(at_ref[2] == 1)
        def _():
            pltpu.make_async_copy(sent, into, sem).start()

        @pl.when(at_ref[2] == 0)
        def _():
            pltpu.make_async_copy(own, into, sem).start()


def place(at_ref, copies, gathered, high_ref, low_ref):
    x, core = at_ref[0], at_ref[1]
    way = 1 - 2 * core
    rows = gathered.shape[1]
    for number in range(8):
        step, other = number % 4, number // 4
        if step == 0:
            copies[other].wait()
        part = core if other == 0 else 1 - core
        chip = lax.rem(x - way * step + 4 if other == 0 else x + way * step + 4, 4)
        start = pl.multiple_of((chip * 2 + part) * rows, rows)
        high, low = split(gathered[number])
        high_ref[pl.ds(start, rows), :] = high
        low_ref[pl.ds(start, rows), :] = low


def fetch_weights(mine, theirs, raw, sem):
    copies = [
        pltpu.make_async_copy(a, raw.at[pl.ds(4 * i, 4)], sem.at[i]) for i, a in enumerate((mine, theirs))
    ]
    for copy in copies:
        copy.start()
    return copies


def frames_kernel(at_ref, own, sent, xh, xl, xt_h, xt_l, x, sem):
    Taken(at_ref, own, sent, x, sem).wait()
    for n in range(x.shape[1] // TILE):
        cut = slice(n * TILE, (n + 1) * TILE)
        high, low = split(x[:, cut])
        xh[:, cut] = high
        xl[:, cut] = low
        xt_h[cut, :] = high.T
        xt_l[cut, :] = low.T


def split_frames(at, own, sent):
    rows, width = own.shape
    shapes = [(rows, width)] * 2 + [(width, rows)] * 2
    return pl.pallas_call(
        frames_kernel,
        in_specs=[SMEM, HBM, HBM],
        out_specs=[VMEM] * 4,
        out_shape=[jax.ShapeDtypeStruct(s, BF16) for s in shapes],
        scratch_shapes=[pltpu.VMEM((rows, width), F32), pltpu.SemaphoreType.DMA],
        name="split_frames",
        **params(rows * width, 6 * 2**20),
    )(at, own, sent)


def first_kernel(scale, at_ref, xh, xl, mine, theirs, hid_h, hid_l, hidt_h, hidt_l, slope, raw, wh, wl, sem):
    place(at_ref, fetch_weights(mine, theirs, raw, sem), raw, wh, wl)
    for n in range(slope.shape[1] // TILE):
        cut = slice(n * TILE, (n + 1) * TILE)
        pre = dot3(xh[...], xl[...], wh[:, cut], wl[:, cut]) * scale
        sig = 1.0 / (1.0 + jnp.exp(-pre))
        hidden = pre * sig
        slope[:, cut] = sig * (1.0 + pre * (1.0 - sig))
        high, low = split(hidden)
        hid_h[:, cut] = high
        hid_l[:, cut] = low
        hidt_h[cut, :] = high.T
        hidt_l[cut, :] = low.T


def first_layer(at, xh, xl, mine, theirs, scale):
    rows, width = xh.shape
    hid = mine.shape[2]
    shapes = [((rows, hid), BF16)] * 2 + [((hid, rows), BF16)] * 2 + [((rows, hid), F32)]
    return pl.pallas_call(
        functools.partial(first_kernel, scale),
        in_specs=[SMEM, VMEM, VMEM, HBM, HBM],
        out_specs=[VMEM] * len(shapes),
        out_shape=[jax.ShapeDtypeStruct(*s) for s in shapes],
        scratch_shapes=[
            pltpu.VMEM((8,) + mine.shape[1:], F32),
            pltpu.VMEM((width, hid), BF16),
            pltpu.VMEM((width, hid), BF16),
            pltpu.SemaphoreType.DMA((2,)),
        ],
        name="first_layer",
        **params(6 * rows * width * hid, 16 * 2**20),
    )(at, xh, xl, mine, theirs)


def second_kernel(scale, at_ref, hid_h, hid_l, mine, theirs, out, wh, wl, raw, sem):
    place(at_ref, fetch_weights(mine, theirs, raw, sem), raw, wh, wl)
    for n in range(out.shape[1] // TILE):
        cut = slice(n * TILE, (n + 1) * TILE)
        out[:, cut] = dot3(hid_h[...], hid_l[...], wh[:, cut], wl[:, cut]) * scale


def second_layer(at, hid_h, hid_l, mine, theirs, scale):
    rows, hid = hid_h.shape
    width = mine.shape[2]
    return pl.pallas_call(
        functools.partial(second_kernel, scale),
        in_specs=[SMEM, VMEM, VMEM, HBM, HBM],
        out_specs=[VMEM] * 3,
        out_shape=[
            jax.ShapeDtypeStruct((rows, width), F32),
            jax.ShapeDtypeStruct((hid, width), BF16),
            jax.ShapeDtypeStruct((hid, width), BF16),
        ],
        scratch_shapes=[pltpu.VMEM((8,) + mine.shape[1:], F32), pltpu.SemaphoreType.DMA((2,))],
        name="second_layer",
        **params(6 * rows * width * hid, 12 * 2**20),
    )(at, hid_h, hid_l, mine, theirs)


def hand_out(at_ref, total, keep, send):
    x, core = at_ref[0], at_ref[1]
    way = 1 - 2 * core
    half = keep.shape[1]
    for k in range(4):
        ahead = lax.rem(x + way * k + 4, 4) * 2
        behind = lax.rem(x - way * k + 4, 4) * 2
        keep[k] = total[pl.ds(pl.multiple_of((ahead + core) * half, half), half), :]
        send[k] = total[pl.ds(pl.multiple_of((behind + 1 - core) * half, half), half), :]


def delta_kernel(frames, scale, begun, start, at_ref, out, own, sent, hidt_h, hidt_l, wh, wl, *refs):
    back_in = refs[0] if begun else None
    keep, send, back, goal, dh, dl, total, sem = refs[1 if begun else 0 :]
    columns = goal.shape[1]
    cut = slice(start, start + columns)
    there = pl.ds(start, columns)
    Taken(at_ref, own.at[:, there], sent.at[:, there], goal, sem).wait()
    high, low = split((out[:, cut] - goal[...]) / frames)
    dh[...] = high
    dl[...] = low
    for n in range(columns // TILE):
        part = slice(n * TILE, (n + 1) * TILE)
        total[:, part] = dot3(hidt_h[...], hidt_l[...], dh[:, part], dl[:, part]) * scale
    hand_out(at_ref, total, keep, send)
    for n in range(back.shape[1] // TILE):
        part = slice(n * TILE, (n + 1) * TILE)
        more = dot3(dh[...], dl[...], wh[part, cut], wl[part, cut], ((1,), (1,)))
        back[:, part] = back_in[:, part] + more if begun else more


def delta_and_second(at, start, columns, out, own, sent, hidt_h, hidt_l, wh, wl, back_in, frames, scale):
    rows = out.shape[0]
    hid = hidt_h.shape[0]
    begun = back_in is not None
    return pl.pallas_call(
        functools.partial(delta_kernel, frames, scale, begun, start),
        in_specs=[SMEM, VMEM, HBM, HBM] + [VMEM] * (5 if begun else 4),
        out_specs=[VMEM] * 3,
        out_shape=[
            jax.ShapeDtypeStruct((4, hid // 8, columns), F32),
            jax.ShapeDtypeStruct((4, hid // 8, columns), F32),
            jax.ShapeDtypeStruct((rows, hid), F32),
        ],
        scratch_shapes=[
            pltpu.VMEM((rows, columns), F32),
            pltpu.VMEM((rows, columns), BF16),
            pltpu.VMEM((rows, columns), BF16),
            pltpu.VMEM((hid, columns), F32),
            pltpu.SemaphoreType.DMA,
        ],
        name="delta_and_second",
        **params(12 * rows * columns * hid, 12 * 2**20),
    )(at, out, own, sent, hidt_h, hidt_l, wh, wl, *([back_in] if begun else []))


def grad_first_kernel(scale_hid, scale_in, start, at_ref, back, slope, xt_h, xt_l, keep, send, total):
    for n in range(total.shape[1] // TILE):
        part = slice(n * TILE, (n + 1) * TILE)
        cut = slice(start + n * TILE, start + (n + 1) * TILE)
        high, low = split((back[:, cut] * scale_hid) * slope[:, cut])
        total[:, part] = dot3(xt_h[...], xt_l[...], high, low) * scale_in
    hand_out(at_ref, total, keep, send)


def grad_first(at, start, columns, back, slope, xt_h, xt_l, scale_hid, scale_in):
    rows, hid = back.shape
    width = xt_h.shape[0]
    return pl.pallas_call(
        functools.partial(grad_first_kernel, scale_hid, scale_in, start),
        in_specs=[SMEM] + [VMEM] * 4,
        out_specs=[VMEM] * 2,
        out_shape=[jax.ShapeDtypeStruct((4, width // 8, columns), F32)] * 2,
        scratch_shapes=[pltpu.VMEM((width, columns), F32)],
        name="grad_first",
        **params(6 * rows * columns * width, 6 * 2**20),
    )(at, back, slope, xt_h, xt_l)


def round_x(a):
    n = lax.axis_size("x")
    pairs = [(i, (i + 1) % n) for i in range(n)] + [(n + i, n + (i - 1) % n) for i in range(n)]
    return lax.ppermute(a, ("core", "x"), pairs)


def to_other_core(a):
    return lax.ppermute(a, "core", [(0, 1), (1, 0)])


def across(a, movers=True, stayers=False):
    places = lax.axis_size("z") * 2

    def index(place, core, y_lo):
        return (place % places) * 4 + core * 2 + y_lo

    pairs = []
    if movers:
        pairs += [(index(i, 0, 1), index(i, 1, 0)) for i in range(places)]
    if stayers:
        pairs += [(index(i, 1, 1), index(i + 1, 0, 0)) for i in range(places)]
    return lax.ppermute(a, ("z", "y_hi", "core", "y_lo"), pairs + [(j, i) for i, j in pairs])


def after(value, *others):
    return lax.optimization_barrier((value, *others))[0]


def body(frames, targets, w_first, w_second):
    inputs, goal = frames[0], targets[0]
    own_first, own_second = w_first[0], w_second[0]
    total_frames = inputs.shape[0] * 8
    width, hid = inputs.shape[1], own_first.shape[1]
    scale_in, scale_hid = width ** (-0.5), hid ** (-0.5)
    half = width // 2
    core = lax.axis_index("core")
    moves = core != lax.axis_index("y_lo")
    at = jnp.stack([lax.axis_index("x"), core, moves]).astype(jnp.int32)

    got_first, got_second = across(own_first, True, True), across(own_second, True, True)
    ring = [jnp.where(moves, got_first, own_first)]
    ring2 = [jnp.where(moves, got_second, own_second)]
    sent = across(after(inputs, got_second))
    sent_goal = across(after(goal, got_second))

    for _ in range(2):
        ring.append(round_x(ring[-1]))
        ring2.append(round_x(ring2[-1]))
    ring.append(round_x(ring[2]))
    xh, xl, xt_h, xt_l = split_frames(at, inputs, sent)
    ring2.append(round_x(after(ring2[2], xh)))
    mine = jnp.stack(ring)
    mine2 = jnp.stack(ring2)
    theirs = to_other_core(mine)
    mine2, sent_goal = lax.optimization_barrier((mine2, sent_goal))
    theirs2 = to_other_core(mine2)

    hid_h, hid_l, hidt_h, hidt_l, slope = first_layer(at, xh, xl, mine, theirs, scale_in)
    got_first, got_second = lax.optimization_barrier((got_first, got_second, hid_h))[:2]
    passed = jnp.stack([to_other_core(got_first), to_other_core(got_second)])
    out, wh, wl = second_layer(at, hid_h, hid_l, mine2, theirs2, scale_hid)

    def delta(start, own, sent, back):
        keep, send, back = delta_and_second(
            at, start, half, out, own, sent, hidt_h, hidt_l, wh, wl, back, total_frames, scale_hid
        )
        return keep, to_other_core(send), back

    def first(start, back):
        keep, send = grad_first(at, start, half, back, slope, xt_h, xt_l, scale_hid, scale_in)
        return keep, to_other_core(send)

    def term(keeps, sents, k):
        return jnp.concatenate([a[k] + b[k] for a, b in zip(keeps, sents)], 1)

    keep0, sent0, back = delta(0, goal, sent_goal, None)
    keep1, sent1, back = delta(half, goal, sent_goal, back)
    second = (keep0, keep1), (sent0, sent1)
    m = term(*second, 3)
    keep2, sent2 = first(0, back)
    keep3, sent3 = first(half, back)
    firsts = (keep2, keep3), (sent2, sent3)
    p = term(*firsts, 3)
    far = across(after(passed, p), False, True)
    m = round_x(m) + term(*second, 2)
    p = round_x(p) + term(*firsts, 2)
    m = round_x(m) + term(*second, 1)
    p = round_x(p) + term(*firsts, 1)
    m = round_x(m) + term(*second, 0)
    far_first, far_second = jnp.where(moves, passed, far) / 3.0
    update_second = far_second - RATE * m
    near_first, near_second = ((w + to_other_core(after(w, back))) / 3.0 for w in (own_first, own_second))
    p, update_second, near_first, near_second, far_first = lax.optimization_barrier(
        (p, update_second, near_first, near_second, far_first)
    )
    p = round_x(p) + term(*firsts, 0)
    update_first = far_first - RATE * p
    new = []
    for near, update in ((near_first, update_first), (near_second, update_second)):
        new.append((near + jnp.where(moves, across(update), update))[None])
    return tuple(new)


def solution(mesh):
    torus = Mesh(
        mesh.devices.reshape(mesh.shape["blk"] // 4, 2, 2, 4, 2), ("z", "y_hi", "core", "x", "y_lo")
    )
    spec = P(("z", "y_hi", "core"), ("x", "y_lo"), None)
    return jax.shard_map(
        body, mesh=torus, in_specs=(spec,) * 4, out_specs=(spec, spec), check_vma=False
    )
```

```python
import functools

import jax
import jax.numpy as jnp
from jax import lax
from jax.experimental import pallas as pl
from jax.experimental.pallas import tpu as pltpu
from jax.sharding import Mesh
from jax.sharding import PartitionSpec as P

RATE = 300.0
F32 = jnp.float32
BF16 = jnp.bfloat16
TILE = 256

VMEM = pl.BlockSpec(memory_space=pltpu.VMEM)
SMEM = pl.BlockSpec(memory_space=pltpu.SMEM)
HBM = pl.BlockSpec(memory_space=pltpu.HBM)


def split(a):
    high = a.astype(BF16)
    return high, (a - high.astype(F32)).astype(BF16)


def dot(a, b, dims=((1,), (0,))):
    return lax.dot_general(a, b, (dims, ((), ())), preferred_element_type=F32)


def dot3(ah, al, bh, bl, dims=((1,), (0,))):
    return dot(ah, bl, dims) + dot(al, bh, dims) + dot(ah, bh, dims)


def params(flops, moved):
    return dict(
        compiler_params=pltpu.CompilerParams(vmem_limit_bytes=30 * 2**20),
        cost_estimate=pl.CostEstimate(flops=flops, bytes_accessed=moved, transcendentals=0),
    )


class Taken:
    def __init__(self, at_ref, own, sent, into, sem):
        self.wait = pltpu.make_async_copy(own, into, sem).wait

        @pl.when(at_ref[2] == 1)
        def _():
            pltpu.make_async_copy(sent, into, sem).start()

        @pl.when(at_ref[2] == 0)
        def _():
            pltpu.make_async_copy(own, into, sem).start()


def place(at_ref, copies, gathered, high_ref, low_ref):
    x, core = at_ref[0], at_ref[1]
    way = 1 - 2 * core
    rows = gathered.shape[1]
    for number in range(8):
        step, other = number % 4, number // 4
        if step == 0:
            copies[other].wait()
        part = core if other == 0 else 1 - core
        chip = lax.rem(x - way * step + 4 if other == 0 else x + way * step + 4, 4)
        start = pl.multiple_of((chip * 2 + part) * rows, rows)
        high, low = split(gathered[number])
        high_ref[pl.ds(start, rows), :] = high
        low_ref[pl.ds(start, rows), :] = low


def fetch_weights(mine, theirs, raw, sem):
    copies = [
        pltpu.make_async_copy(a, raw.at[pl.ds(4 * i, 4)], sem.at[i]) for i, a in enumerate((mine, theirs))
    ]
    for copy in copies:
        copy.start()
    return copies


def frames_kernel(at_ref, own, sent, xh, xl, xt_h, xt_l, x, sem):
    Taken(at_ref, own, sent, x, sem).wait()
    for n in range(x.shape[1] // TILE):
        cut = slice(n * TILE, (n + 1) * TILE)
        high, low = split(x[:, cut])
        xh[:, cut] = high
        xl[:, cut] = low
        xt_h[cut, :] = high.T
        xt_l[cut, :] = low.T


def split_frames(at, own, sent):
    rows, width = own.shape
    shapes = [(rows, width)] * 2 + [(width, rows)] * 2
    return pl.pallas_call(
        frames_kernel,
        in_specs=[SMEM, HBM, HBM],
        out_specs=[VMEM] * 4,
        out_shape=[jax.ShapeDtypeStruct(s, BF16) for s in shapes],
        scratch_shapes=[pltpu.VMEM((rows, width), F32), pltpu.SemaphoreType.DMA],
        name="split_frames",
        **params(rows * width, 6 * 2**20),
    )(at, own, sent)


def first_kernel(scale, at_ref, xh, xl, mine, theirs, hid_h, hid_l, hidt_h, hidt_l, slope, raw, wh, wl, sem):
    place(at_ref, fetch_weights(mine, theirs, raw, sem), raw, wh, wl)
    for n in range(slope.shape[1] // TILE):
        cut = slice(n * TILE, (n + 1) * TILE)
        pre = dot3(xh[...], xl[...], wh[:, cut], wl[:, cut]) * scale
        sig = 1.0 / (1.0 + jnp.exp(-pre))
        hidden = pre * sig
        slope[:, cut] = sig * (1.0 + pre * (1.0 - sig))
        high, low = split(hidden)
        hid_h[:, cut] = high
        hid_l[:, cut] = low
        hidt_h[cut, :] = high.T
        hidt_l[cut, :] = low.T


def first_layer(at, xh, xl, mine, theirs, scale):
    rows, width = xh.shape
    hid = mine.shape[2]
    shapes = [((rows, hid), BF16)] * 2 + [((hid, rows), BF16)] * 2 + [((rows, hid), F32)]
    return pl.pallas_call(
        functools.partial(first_kernel, scale),
        in_specs=[SMEM, VMEM, VMEM, HBM, HBM],
        out_specs=[VMEM] * len(shapes),
        out_shape=[jax.ShapeDtypeStruct(*s) for s in shapes],
        scratch_shapes=[
            pltpu.VMEM((8,) + mine.shape[1:], F32),
            pltpu.VMEM((width, hid), BF16),
            pltpu.VMEM((width, hid), BF16),
            pltpu.SemaphoreType.DMA((2,)),
        ],
        name="first_layer",
        **params(6 * rows * width * hid, 16 * 2**20),
    )(at, xh, xl, mine, theirs)


def second_kernel(scale, at_ref, hid_h, hid_l, mine, theirs, out, wh, wl, raw, sem):
    place(at_ref, fetch_weights(mine, theirs, raw, sem), raw, wh, wl)
    for n in range(out.shape[1] // TILE):
        cut = slice(n * TILE, (n + 1) * TILE)
        out[:, cut] = dot3(hid_h[...], hid_l[...], wh[:, cut], wl[:, cut]) * scale


def second_layer(at, hid_h, hid_l, mine, theirs, scale):
    rows, hid = hid_h.shape
    width = mine.shape[2]
    return pl.pallas_call(
        functools.partial(second_kernel, scale),
        in_specs=[SMEM, VMEM, VMEM, HBM, HBM],
        out_specs=[VMEM] * 3,
        out_shape=[
            jax.ShapeDtypeStruct((rows, width), F32),
            jax.ShapeDtypeStruct((hid, width), BF16),
            jax.ShapeDtypeStruct((hid, width), BF16),
        ],
        scratch_shapes=[pltpu.VMEM((8,) + mine.shape[1:], F32), pltpu.SemaphoreType.DMA((2,))],
        name="second_layer",
        **params(6 * rows * width * hid, 12 * 2**20),
    )(at, hid_h, hid_l, mine, theirs)


def hand_out(at_ref, total, keep, send):
    x, core = at_ref[0], at_ref[1]
    way = 1 - 2 * core
    half = keep.shape[1]
    for k in range(4):
        ahead = lax.rem(x + way * k + 4, 4) * 2
        behind = lax.rem(x - way * k + 4, 4) * 2
        keep[k] = total[pl.ds(pl.multiple_of((ahead + core) * half, half), half), :]
        send[k] = total[pl.ds(pl.multiple_of((behind + 1 - core) * half, half), half), :]


def delta_kernel(frames, scale, begun, start, at_ref, out, own, sent, hidt_h, hidt_l, wh, wl, *refs):
    back_in = refs[0] if begun else None
    keep, send, back, goal, dh, dl, total, sem = refs[1 if begun else 0 :]
    columns = goal.shape[1]
    cut = slice(start, start + columns)
    there = pl.ds(start, columns)
    Taken(at_ref, own.at[:, there], sent.at[:, there], goal, sem).wait()
    high, low = split((out[:, cut] - goal[...]) / frames)
    dh[...] = high
    dl[...] = low
    for n in range(columns // TILE):
        part = slice(n * TILE, (n + 1) * TILE)
        total[:, part] = dot3(hidt_h[...], hidt_l[...], dh[:, part], dl[:, part]) * scale
    hand_out(at_ref, total, keep, send)
    for n in range(back.shape[1] // TILE):
        part = slice(n * TILE, (n + 1) * TILE)
        more = dot3(dh[...], dl[...], wh[part, cut], wl[part, cut], ((1,), (1,)))
        back[:, part] = back_in[:, part] + more if begun else more


def delta_and_second(at, start, columns, out, own, sent, hidt_h, hidt_l, wh, wl, back_in, frames, scale):
    rows = out.shape[0]
    hid = hidt_h.shape[0]
    begun = back_in is not None
    return pl.pallas_call(
        functools.partial(delta_kernel, frames, scale, begun, start),
        in_specs=[SMEM, VMEM, HBM, HBM] + [VMEM] * (5 if begun else 4),
        out_specs=[VMEM] * 3,
        out_shape=[
            jax.ShapeDtypeStruct((4, hid // 8, columns), F32),
            jax.ShapeDtypeStruct((4, hid // 8, columns), F32),
            jax.ShapeDtypeStruct((rows, hid), F32),
        ],
        scratch_shapes=[
            pltpu.VMEM((rows, columns), F32),
            pltpu.VMEM((rows, columns), BF16),
            pltpu.VMEM((rows, columns), BF16),
            pltpu.VMEM((hid, columns), F32),
            pltpu.SemaphoreType.DMA,
        ],
        name="delta_and_second",
        **params(12 * rows * columns * hid, 12 * 2**20),
    )(at, out, own, sent, hidt_h, hidt_l, wh, wl, *([back_in] if begun else []))


def grad_first_kernel(scale_hid, scale_in, start, at_ref, back, slope, xt_h, xt_l, keep, send, total):
    for n in range(total.shape[1] // TILE):
        part = slice(n * TILE, (n + 1) * TILE)
        cut = slice(start + n * TILE, start + (n + 1) * TILE)
        high, low = split((back[:, cut] * scale_hid) * slope[:, cut])
        total[:, part] = dot3(xt_h[...], xt_l[...], high, low) * scale_in
    hand_out(at_ref, total, keep, send)


def grad_first(at, start, columns, back, slope, xt_h, xt_l, scale_hid, scale_in):
    rows, hid = back.shape
    width = xt_h.shape[0]
    return pl.pallas_call(
        functools.partial(grad_first_kernel, scale_hid, scale_in, start),
        in_specs=[SMEM] + [VMEM] * 4,
        out_specs=[VMEM] * 2,
        out_shape=[jax.ShapeDtypeStruct((4, width // 8, columns), F32)] * 2,
        scratch_shapes=[pltpu.VMEM((width, columns), F32)],
        name="grad_first",
        **params(6 * rows * columns * width, 6 * 2**20),
    )(at, back, slope, xt_h, xt_l)


def round_x(a):
    n = lax.axis_size("x")
    pairs = [(i, (i + 1) % n) for i in range(n)] + [(n + i, n + (i - 1) % n) for i in range(n)]
    return lax.ppermute(a, ("core", "x"), pairs)


def to_other_core(a):
    return lax.ppermute(a, "core", [(0, 1), (1, 0)])


def across(a, movers=True, stayers=False):
    places = lax.axis_size("z") * 2

    def index(place, core, y_lo):
        return (place % places) * 4 + core * 2 + y_lo

    pairs = []
    if movers:
        pairs += [(index(i, 0, 1), index(i, 1, 0)) for i in range(places)]
    if stayers:
        pairs += [(index(i, 1, 1), index(i + 1, 0, 0)) for i in range(places)]
    return lax.ppermute(a, ("z", "y_hi", "core", "y_lo"), pairs + [(j, i) for i, j in pairs])


def after(value, *others):
    return lax.optimization_barrier((value, *others))[0]


def body(frames, targets, w_first, w_second):
    inputs, goal = frames[0], targets[0]
    own_first, own_second = w_first[0], w_second[0]
    total_frames = inputs.shape[0] * 8
    width, hid = inputs.shape[1], own_first.shape[1]
    scale_in, scale_hid = width ** (-0.5), hid ** (-0.5)
    half = width // 2
    core = lax.axis_index("core")
    moves = core != lax.axis_index("y_lo")
    at = jnp.stack([lax.axis_index("x"), core, moves]).astype(jnp.int32)

    got_first, got_second = across(own_first, True, True), across(own_second, True, True)
    ring = [jnp.where(moves, got_first, own_first)]
    ring2 = [jnp.where(moves, got_second, own_second)]
    sent = across(after(inputs, got_second))
    sent_goal = across(after(goal, got_second))

    for _ in range(2):
        ring.append(round_x(ring[-1]))
        ring2.append(round_x(ring2[-1]))
    ring.append(round_x(ring[2]))
    xh, xl, xt_h, xt_l = split_frames(at, inputs, sent)
    ring2.append(round_x(after(ring2[2], xh)))
    mine = jnp.stack(ring)
    mine2 = jnp.stack(ring2)
    theirs = to_other_core(mine)
    mine2, sent_goal = lax.optimization_barrier((mine2, sent_goal))
    theirs2 = to_other_core(mine2)

    hid_h, hid_l, hidt_h, hidt_l, slope = first_layer(at, xh, xl, mine, theirs, scale_in)
    got_first, got_second = lax.optimization_barrier((got_first, got_second, hid_h))[:2]
    passed = jnp.stack([to_other_core(got_first), to_other_core(got_second)])
    out, wh, wl = second_layer(at, hid_h, hid_l, mine2, theirs2, scale_hid)

    def delta(start, own, sent, back):
        keep, send, back = delta_and_second(
            at, start, half, out, own, sent, hidt_h, hidt_l, wh, wl, back, total_frames, scale_hid
        )
        return keep, to_other_core(send), back

    def first(start, back):
        keep, send = grad_first(at, start, width, back, slope, xt_h, xt_l, scale_hid, scale_in)
        return keep, to_other_core(send)

    def term(keeps, sents, k):
        return jnp.concatenate([a[k] + b[k] for a, b in zip(keeps, sents)], 1)

    keep0, sent0, back = delta(0, goal, sent_goal, None)
    keep1, sent1, back = delta(half, goal, sent_goal, back)
    second = (keep0, keep1), (sent0, sent1)
    m = term(*second, 3)
    keep2, sent2 = first(0, back)
    firsts = (keep2,), (sent2,)
    p = term(*firsts, 3)
    far = across(after(passed, p), False, True)
    m = round_x(m) + term(*second, 2)
    p = round_x(p) + term(*firsts, 2)
    m = round_x(m) + term(*second, 1)
    p = round_x(p) + term(*firsts, 1)
    m = round_x(m) + term(*second, 0)
    far_first, far_second = jnp.where(moves, passed, far) / 3.0
    update_second = far_second - RATE * m
    near_first, near_second = ((w + to_other_core(after(w, back))) / 3.0 for w in (own_first, own_second))
    p, update_second, near_first, near_second, far_first = lax.optimization_barrier(
        (p, update_second, near_first, near_second, far_first)
    )
    p = round_x(p) + term(*firsts, 0)
    update_first = far_first - RATE * p
    new = []
    for near, update in ((near_first, update_first), (near_second, update_second)):
        new.append((near + jnp.where(moves, across(update), update))[None])
    return tuple(new)


def solution(mesh):
    torus = Mesh(
        mesh.devices.reshape(mesh.shape["blk"] // 4, 2, 2, 4, 2), ("z", "y_hi", "core", "x", "y_lo")
    )
    spec = P(("z", "y_hi", "core"), ("x", "y_lo"), None)
    return jax.shard_map(
        body, mesh=torus, in_specs=(spec,) * 4, out_specs=(spec, spec), check_vma=False
    )
```
